512 devices in a mesh: ep: 128 (over z, x, core), tp: 4 (over y).
Axes of the slice: x: 4, y: 4, z: 16, core: 2. Of those that a mesh axis runs over, the one named last changes fastest.
Arguments:
- grad_out: bfloat16 [16384, 4096], P('ep', 'tp'), may hold values from -6 to 6
- routes: int32 [16384, 8], P('ep'), may hold values from 0 to 127, all different within a row; in each aligned block of 128 rows (0 to 127, 128 to 255, ...) at most 16 rows name the same one
- combine: float32 [16384, 8], P('ep'), may hold values from 0.05 to 0.5
- gate_act: bfloat16 [16384, 8, 768], P('ep', None, 'tp'), may hold values from -6 to 6
- up_act: bfloat16 [16384, 8, 768], P('ep', None, 'tp'), may hold values from -6 to 6
- w_down: bfloat16 [128, 768, 4096], P('ep', None, 'tp'), may hold values from -0.21875 to 0.21875
Outputs:
- w_down_grad: bfloat16 [128, 768, 4096], P('ep', None, 'tp')
- gate_grad: bfloat16 [16384, 8, 768], P('ep', None, 'tp')
- up_grad: bfloat16 [16384, 8, 768], P('ep', None, 'tp')
- combine_grad: float32 [16384, 8], P('ep')
The draws below stay inside these ranges and needn't reach their ends.
Inputs may be any that keep to these rules, and one draw needn't show every extreme that they name: `routes`: each row names 8 different experts. Among the rows of one index of ep (aligned blocks of 128 tokens) no expert is named more than 16 times, and in every draw some expert is named exactly 16 times in some such block.
All inputs are finite; a program needn't handle non-finite values.
Results may differ from the reference program's by a relative error of at most 0.015.
Values may be sent and summed in bfloat16 or wider, within the bound.
A program may use at most 64 MiB of HBM per device.

```python
import math
import jax
import jax.numpy as jnp
import numpy as np
from jax import lax

D = 4096
FF = 768
TOPK = 8
TOK_DEV = 128
EXPERTS = 128
TOKENS = 16384
CAP = 16
N_TP = 4


def levels(stream_key, dims, cuts, least, top_value):
    def one(position, parts):
        draws = jax.random.uniform(jax.random.fold_in(jax.random.fold_in(stream_key, 6), position), (parts,), jnp.float32, least / len(cuts), top_value / len(cuts))
        return jnp.repeat(jnp.exp(draws), dims[position] // parts).reshape((-1,) + (1,) * (len(dims) - position - 1))

    factor_of = one(*cuts[0])
    for cut in cuts[1:]:
        factor_of = factor_of * one(*cut)
    return factor_of


def deal_out(rng, own, number, rows, amount, top, reach, slope):
    order = jax.random.permutation(rng, amount)
    crowded, usual = portions_of(amount, rows * top, reach, slope, True), portions_of(amount, rows * top, reach, slope, False)
    places = jnp.arange(amount)

    def named(sizes, turn):
        used = int((sizes > 0).sum())
        fixed = max(1, used // 4)
        passed = fixed + (places - fixed + turn * (used - fixed)) % max(1, amount - fixed)
        return jnp.zeros((amount,), jnp.int32).at[order[jnp.where(places < fixed, places, passed)]].set(jnp.asarray(sizes, jnp.int32))

    sizes = jnp.where(number % 4 == 0, named(crowded, number // 4), named(usual, number - number // 4 - 1))
    mixed = jax.random.permutation(jax.random.fold_in(own, 3), amount)
    donor, sink = mixed[0:amount // 2 * 2:2], mixed[1:amount // 2 * 2:2]
    margin = jnp.minimum(sizes[donor] - 1, reach - sizes[sink]) // 2
    margin = jnp.where((donor == order[0]) | (sink == order[0]) | (sizes[sink] == 0), 0, jnp.maximum(margin, 0))
    passed = jax.random.randint(jax.random.fold_in(own, 4), (amount // 2,), 0, 1 << 20) % (margin + 1)
    sizes = sizes.at[donor].add(-passed).at[sink].add(passed)
    items = jnp.searchsorted(jnp.cumsum(sizes), jnp.arange(rows * top), side="right").astype(jnp.int32)
    grid = items.reshape(top, rows).T
    grid = grid[jax.random.permutation(jax.random.fold_in(own, 1), rows)]
    turn = jax.random.randint(jax.random.fold_in(own, 2), (rows, 1), 0, top)
    return jnp.take_along_axis(grid, (jnp.arange(top)[None, :] + turn) % top, axis=1)


def portions_of(number_of, total, reach, lean, full):
    loads = [(1 << 20) // math.isqrt(standing ** lean) + 1 for standing in range(1, number_of + 1)]
    largest = reach if full else min(reach, max(-(-total // number_of), total * loads[0] // sum(loads)))
    least = 1 if total - largest >= number_of - 1 else 0
    holding, surplus = [largest] + [least] * (number_of - 1), total - largest - least * (number_of - 1)
    while surplus > 0:
        movable = [i for i in range(1, number_of) if holding[i] < largest] or [i for i in range(1, number_of) if holding[i] < reach]
        whole, left = sum([loads[i] for i in movable]), surplus
        for i in movable:
            addition = min(reach - holding[i], max(1, left * loads[i] // whole), surplus)
            holding[i] = holding[i] + addition
            surplus = surplus - addition
    return np.array(holding)


def scatter_about(stream_key, extent, spread, most, shards=(), held_as=jnp.bfloat16):
    array = jax.random.normal(stream_key, extent, jnp.float32) * spread
    if len(shards) > 0:
        array = levels(stream_key, extent, shards, -0.22, 0.18) * array
    return jnp.clip(array, min=-most, max=most).astype(held_as)


def setup_inputs(seed: int = 0) -> dict:
    splits = jax.random.split(jax.random.key(seed), 7)
    grad_out = scatter_about(splits[0], (TOKENS, D), 1.0, 6.0, ((0, 128), (1, 4)))
    routes_keys = jax.random.split(jax.random.fold_in(splits[1], 1), TOKENS // TOK_DEV)
    routes_turns = jax.random.permutation(jax.random.fold_in(splits[1], 3), TOKENS // TOK_DEV)
    routes = jax.vmap(lambda own, number: deal_out(jax.random.fold_in(splits[1], 2), own, number, TOK_DEV, EXPERTS, TOPK, CAP, 2))(routes_keys, routes_turns).reshape((TOKENS, TOPK))
    combine = jnp.clip(jnp.exp(math.log(0.5) - 2.3025851 * jax.random.uniform(splits[2], (TOKENS, TOPK), jnp.float32) ** levels(splits[2], (TOKENS, TOPK), ((0, 128),), -0.2, 0.2)), 0.05, 0.5)
    gate_act = scatter_about(splits[3], (TOKENS, TOPK, FF), 1.0, 6.0, ((0, 128), (2, 4)))
    up_act = scatter_about(splits[4], (TOKENS, TOPK, FF), 1.0, 6.0, ((0, 128), (2, 4)))
    w_down = scatter_about(splits[5], (EXPERTS, FF, D), FF ** -0.5, 0.21875, ((0, 128), (2, 4)))
    return {"grad_out": grad_out, "routes": routes, "combine": combine, "gate_act": gate_act, "up_act": up_act, "w_down": w_down}


def reference(grad_out, routes, combine, gate_act, up_act, w_down):
    all_rows = TOKENS * TOPK
    feat_local = D // N_TP
    gate_flat = gate_act.reshape(all_rows, FF).astype(jnp.float32)
    up_flat = up_act.reshape(all_rows, FF).astype(jnp.float32)
    sigmoid_gate = jax.nn.sigmoid(gate_flat)
    silu_gate = gate_flat * sigmoid_gate
    hidden = silu_gate * up_flat
    weights_flat = combine.reshape(all_rows).astype(jnp.float32)
    weighted = (weights_flat[:, None] * hidden).astype(jnp.bfloat16)
    flat_routes = routes.reshape(all_rows).astype(jnp.int32)
    ordering = jnp.argsort(flat_routes, stable=True).astype(jnp.int32)
    expert_ids = jnp.arange(EXPERTS, dtype=jnp.int32)
    counts = jnp.sum((flat_routes[:, None] == expert_ids[None, :]).astype(jnp.int32), axis=0).astype(jnp.int32)
    starts = (jnp.cumsum(counts) - counts).astype(jnp.int32)
    most_rows = EXPERTS * CAP
    ordering = jnp.concatenate([ordering, jnp.full((most_rows,), all_rows, jnp.int32)])
    grad_padded = jnp.concatenate([grad_out, jnp.zeros((1, D), grad_out.dtype)], axis=0)
    weighted_padded = jnp.concatenate([weighted, jnp.zeros((1, FF), weighted.dtype)], axis=0)
    slot_ids = jnp.arange(most_rows, dtype=jnp.int32)

    def expert_step(carry, expert):
        members = lax.dynamic_slice(ordering, (starts[expert],), (most_rows,))
        members = jnp.where(slot_ids < counts[expert], members, all_rows).astype(jnp.int32)
        grad_rows = grad_padded[members // TOPK]
        weighted_rows = weighted_padded[members]
        down_grad = jnp.dot(weighted_rows.T, grad_rows, preferred_element_type=jnp.float32).astype(jnp.bfloat16)
        weight_now = w_down[expert]
        total = jnp.zeros((most_rows, FF), jnp.float32)
        for part_index in range(N_TP):
            lower = part_index * feat_local
            upper = lower + feat_local
            term = jnp.dot(grad_rows[:, lower:upper], weight_now[:, lower:upper].T, preferred_element_type=jnp.float32)
            rounded = lax.optimization_barrier(term.astype(jnp.bfloat16))
            total = total + rounded.astype(jnp.float32)
        carry = carry.at[members].set(total)
        return carry, down_grad

    raw_init = jnp.zeros((all_rows + 1, FF), jnp.float32)
    raw_all, w_down_grad = lax.scan(expert_step, raw_init, expert_ids)
    raw_hidden = raw_all[:all_rows]
    combine_grad = jnp.sum(hidden * raw_hidden, axis=1).reshape(TOKENS, TOPK)
    scaled = weights_flat[:, None] * raw_hidden
    gate_grad = (scaled * up_flat * sigmoid_gate * (1.0 + gate_flat * (1.0 - sigmoid_gate))).astype(jnp.bfloat16)
    up_grad = (scaled * silu_gate).astype(jnp.bfloat16)
    return (w_down_grad, gate_grad.reshape(TOKENS, TOPK, FF), up_grad.reshape(TOKENS, TOPK, FF), combine_grad)
```

```python
import functools

import jax
import jax.numpy as jnp
from jax import lax
from jax.experimental import pallas as pl
from jax.experimental.pallas import tpu as pltpu
from jax.sharding import PartitionSpec as P

MESH = pl.DeviceIdType.MESH
NT = (((1,), (1,)), ((), ()))


def regroup(blocks, cap):
    count = len(blocks)
    lane = lax.broadcasted_iota(jnp.int32, blocks[0].shape, 1)
    lanes = blocks[0].shape[1]
    bit = 1
    while bit < count:
        high = (lane & (bit * cap)) != 0
        fresh = list(blocks)
        for low in range(count):
            if low & bit:
                continue
            a, b = blocks[low], blocks[low | bit]
            fresh[low] = jnp.where(high, pltpu.roll(b, bit * cap, 1), a)
            fresh[low | bit] = jnp.where(high, b, pltpu.roll(a, lanes - bit * cap, 1))
        blocks = fresh
        bit *= 2
    return blocks


def kernel(
    nz, nxc, ntp, cap,
    grad, routes_t, routes_c, combine_c, gate, up, w,
    wgrad, gate_out, up_out, cg_out,
    zbuf, sbuf, xs, rows, hs, rs, zsend, zret, wx, wxr, wz, wt, xsend, ret, pick, wtok, rank, cgp, cgr,
    zg_s, zg_r, sl_s, sl_r, xs_s, xs_r, rs_s, rs_r, zr_s, zr_r, wx_s, wx_r, wz_s, wz_r, wy_s, wy_r,
    rx_s, rx_r, cg_s, cg_r,
):
    tokens, feats = grad.shape
    top = routes_t.shape[0]
    units = gate.shape[2]
    experts = nz * nxc
    block = nxc * cap
    wide = nz * cap
    half_z = nz // 2
    half_t = tokens // 2
    tile_t = min(16, tokens)
    tile_r = tile_t * top
    tiles = tokens // tile_t

    ep, y = lax.axis_index("ep"), lax.axis_index("tp")
    z, xc = ep // nxc, ep % nxc

    def at_z(other):
        return (other * nxc + xc, y)

    def at_xc(other):
        return (z * nxc + other, y)

    def at_y(other):
        return (ep, other)

    def remote(src, dst, send, recv, device):
        return pltpu.make_async_remote_copy(
            src_ref=src, dst_ref=dst, send_sem=send, recv_sem=recv, device_id=device,
            device_id_type=MESH,
        )

    def drain(ref, sem):
        pltpu.make_async_copy(ref, ref, sem).wait()

    def lanes_of(index):
        return pl.ds(pl.multiple_of(index * block, block), block)

    def rows_of(index):
        return pl.ds(pl.multiple_of(index * cap, cap), cap)

    barrier = pltpu.get_barrier_semaphore()

    def greet(count, me, place):
        def one(d, _):
            pl.semaphore_signal(
                barrier, inc=1, device_id=place((me + d) % count), device_id_type=MESH
            )
            return 0

        lax.fori_loop(1, count, one, 0)

    greet(nz, z, at_z)
    greet(nxc, xc, at_xc)
    greet(ntp, y, at_y)
    pl.semaphore_wait(barrier, nz + nxc + ntp - 3)

    ahead = ((z + 1) % nz, (z + nz - 1) % nz)

    def ring(src, source, direction, step, part):
        span = pl.ds(part * half_t, half_t)
        return remote(
            src.at[span], zbuf.at[source, span], zg_s.at[direction, step, part],
            zg_r.at[direction, step, part], at_z(ahead[direction]),
        )

    def ring_slots(src, source, direction, step):
        return remote(
            src, sbuf.at[source], sl_s.at[direction, step], sl_r.at[direction, step],
            at_z(ahead[direction]),
        )

    for part in range(2):
        for direction in range(2):
            ring(grad, z, direction, 0, part).start()

    expert_of = lax.broadcasted_iota(jnp.int32, (experts, tokens), 0)
    named = jnp.zeros((experts, tokens), jnp.float32)
    for k in range(top):
        named = named + jnp.where(routes_t[k : k + 1, :] == expert_of, 1.0, 0.0)
    before = lax.broadcasted_iota(jnp.int32, (tokens, tokens), 0) < lax.broadcasted_iota(
        jnp.int32, (tokens, tokens), 1
    )
    rank_t = jnp.dot(
        named.astype(jnp.bfloat16),
        jnp.where(before, 1.0, 0.0).astype(jnp.bfloat16),
        preferred_element_type=jnp.float32,
    )
    code = rank_t + (expert_of * cap).astype(jnp.float32)
    for k in range(top):
        picked = jnp.where(routes_t[k : k + 1, :] == expert_of, code, 0.0)
        sbuf[z, k : k + 1, :] = jnp.sum(picked, axis=0, keepdims=True).astype(jnp.int32)
    for direction in range(2):
        ring_slots(sbuf.at[z], z, direction, 0).start()
    rank[...] = rank_t.T

    def weigh(i, _):
        span = pl.ds(i * tile_t, tile_t)
        flat = pl.ds(pl.multiple_of(i * tile_r, tile_r), tile_r)
        lane = lax.broadcasted_iota(jnp.int32, (tile_r, experts), 1)
        base = ((lane % nxc) * wide + (lane // nxc) * cap).astype(jnp.float32)
        mine = jnp.broadcast_to(
            rank[span][:, None, :], (tile_t, top, experts)
        ).reshape(tile_r, experts)
        slot = jnp.sum(
            jnp.where(routes_c[flat] == lane, mine + base, 0.0), axis=1, keepdims=True
        ).astype(jnp.int32)
        for other in range(nxc):
            at = lax.broadcasted_iota(jnp.int32, (tile_r, wide), 1) + other * wide
            pick[flat, other * wide : (other + 1) * wide] = jnp.where(
                slot == at, 1.0, 0.0
            ).astype(jnp.bfloat16)
        g = gate[span].astype(jnp.float32).reshape(tile_r, units)
        u = up[span].astype(jnp.float32).reshape(tile_r, units)
        s = 1.0 / (1.0 + jnp.exp(-g))
        weighted = combine_c[flat] * (g * s * u)
        wtok[:, flat] = weighted.T.astype(jnp.bfloat16)
        return 0

    lax.fori_loop(0, tiles, weigh, 0)

    def place_weighted(d, _):
        other = (xc + d) % nxc
        span = pl.ds(pl.multiple_of(other * wide, wide), wide)
        value = jnp.dot(
            wtok[...], pick[:, span], preferred_element_type=jnp.float32
        ).astype(jnp.bfloat16)

        @pl.when(d > 0)
        def _():
            wx[other] = value
            remote(wx.at[other], wxr.at[xc], wx_s, wx_r, at_xc(other)).start()

        @pl.when(d == 0)
        def _():
            wxr[xc] = value

        return 0

    lax.fori_loop(0, nxc, place_weighted, 0)

    def deal(source, chunk):
        at = lax.broadcasted_iota(jnp.int32, (block, tokens), 0) + z * block
        chosen = sbuf[source, 0:1, :] == at
        for k in range(1, top):
            chosen = chosen | (sbuf[source, k : k + 1, :] == at)
        select = jnp.where(chosen, 1.0, 0.0).astype(jnp.bfloat16)
        piece = min(256, feats)
        for lo in range(0, feats, piece):
            xs[source, :, lo : lo + piece] = jnp.dot(
                select, chunk[:, lo : lo + piece], preferred_element_type=jnp.float32
            ).astype(jnp.bfloat16)
        rows[source, rows_of(xc), :] = xs[source, rows_of(xc), :]

        def send(d, _):
            other = (xc + d) % nxc
            remote(
                xs.at[source, rows_of(other)], rows.at[source, rows_of(xc)],
                xs_s.at[source], xs_r.at[source], at_xc(other),
            ).start()
            return 0

        lax.fori_loop(1, nxc, send, 0)

    def project(source):
        drain(rows.at[source, pl.ds(0, block - cap)], xs_r.at[source])
        for d in range(ntp):
            other = (y + d) % ntp
            weights = w[0, pl.ds(pl.multiple_of(other * units, units), units), :]
            value = lax.dot_general(
                weights, rows[source], NT, preferred_element_type=jnp.float32
            ).astype(jnp.bfloat16)
            if d == 0:
                rs[source, y] = value
            else:
                hs[source, d - 1] = value
                remote(
                    hs.at[source, d - 1], rs.at[source, y], rs_s.at[source], rs_r.at[source],
                    at_y(other),
                ).start()

    def total(source):
        drain(rs.at[source, pl.ds(0, ntp - 1)], rs_r.at[source])
        out = rs[source, 0].astype(jnp.float32)
        for q in range(1, ntp):
            out = out + rs[source, q].astype(jnp.float32)
        return out.astype(jnp.bfloat16)

    def give_back(source):
        zsend[source] = total(source)
        remote(
            zsend.at[source], zret.at[z], zr_s.at[source], zr_r.at[z], at_z(source)
        ).start()

    def below(step):
        return (z + nz - step) % nz

    def above(step):
        return (z + step) % nz

    def both(step, act):
        act(below(step))
        act(above(step))

    deal(z, grad)

    def gather_step(step, _):
        sources = (below(step), above(step))
        for part in range(2):
            for direction in range(2):
                source = sources[direction]
                ring(zbuf.at[source], source, direction, step - 1, part).wait_recv()
                if part == direction:
                    ring(zbuf.at[source], source, direction, step, part).start()
                else:

                    @pl.when(step < half_z - 1)
                    def _():
                        ring(zbuf.at[source], source, direction, step, part).start()

        for direction in range(2):
            source = sources[direction]
            ring_slots(sbuf.at[source], source, direction, step - 1).wait_recv()
            if direction == 0:
                ring_slots(sbuf.at[source], source, direction, step).start()
            else:

                @pl.when(step < half_z - 1)
                def _():
                    ring_slots(sbuf.at[source], source, direction, step).start()

        for direction in range(2):
            deal(sources[direction], zbuf.at[sources[direction]])

        @pl.when(step == 1)
        def _():
            project(z)

        @pl.when(step > 1)
        def _():
            both(step - 1, project)

        @pl.when(step == 2)
        def _():
            zret[z] = total(z)

        @pl.when(step > 2)
        def _():
            both(step - 2, give_back)

        return 0

    lax.fori_loop(1, half_z, gather_step, 0)

    far = above(half_z)
    for direction in range(2):
        ring(zbuf.at[far], far, direction, half_z - 1, direction).wait_recv()
    ring_slots(sbuf.at[far], far, 0, half_z - 1).wait_recv()
    deal(far, zbuf.at[far])

    drain(wxr.at[pl.ds(0, nxc - 1)], wx_r)
    strip = 16 if units % 16 == 0 else units

    def regroup_weighted(i, _):
        span = pl.ds(pl.multiple_of(i * strip, strip), strip)
        for part in range(nz // nxc):
            blocks = [
                wxr[other, span, part * block : (part + 1) * block].astype(jnp.float32)
                for other in range(nxc)
            ]
            for low, value in enumerate(regroup(blocks, cap)):
                wz[part * nxc + low, span, :] = value.astype(jnp.bfloat16)
        return 0

    lax.fori_loop(0, units // strip, regroup_weighted, 0)

    def send_weighted(d, _):
        other = (z + d) % nz
        remote(
            wz.at[other], wt.at[y, :, lanes_of(z)], wz_s.at[other], wz_r.at[z], at_z(other)
        ).start()
        return 0

    lax.fori_loop(1, nz, send_weighted, 0)
    wt[y, :, lanes_of(z)] = wz[z]

    both(half_z - 1, project)
    both(half_z - 2, give_back) if half_z > 2 else None
    project(far)
    both(half_z - 1, give_back)
    give_back(far)

    def spread_weighted(d, _):
        source = (z + d) % nz

        @pl.when(d > 0)
        def _():
            drain(wt.at[y, :, lanes_of(source)], wz_r.at[source])

        for e in range(1, ntp):
            remote(
                wt.at[y, :, lanes_of(source)], wt.at[y, :, lanes_of(source)], wy_s, wy_r,
                at_y((y + e) % ntp),
            ).start()
        return 0

    lax.fori_loop(0, nz, spread_weighted, 0)
    drain(wt.at[pl.ds(0, ntp - 1)], wy_r)

    piece = min(256, feats)
    per = feats // piece

    def weight_gradient(i, _):
        q, n = i // per, i % per
        cols = pl.ds(pl.multiple_of(n * piece, piece), piece)
        wgrad[0, pl.ds(pl.multiple_of(q * units, units), units), cols] = jnp.dot(
            wt[q],
            rows[:, :, cols].reshape(nz * block, piece),
            preferred_element_type=jnp.float32,
        ).astype(jnp.bfloat16)
        return 0

    lax.fori_loop(0, ntp * per, weight_gradient, 0)

    def await_back(d, _):
        source = (z + d) % nz
        drain(zret.at[source], zr_r.at[source])
        return 0

    lax.fori_loop(1, nz, await_back, 0)

    def regroup_back(i, _):
        span = pl.ds(pl.multiple_of(i * strip, strip), strip)
        for part in range(nz // nxc):
            blocks = [
                zret[part * nxc + low, span, :].astype(jnp.float32) for low in range(nxc)
            ]
            for other, value in enumerate(regroup(blocks, cap)):
                xsend[other, span, part * block : (part + 1) * block] = value.astype(jnp.bfloat16)
        return 0

    lax.fori_loop(0, units // strip, regroup_back, 0)

    def send_back(d, _):
        other = (xc + d) % nxc
        remote(xsend.at[other], ret.at[xc], rx_s, rx_r, at_xc(other)).start()
        return 0

    lax.fori_loop(1, nxc, send_back, 0)
    ret[xc] = xsend[xc]
    drain(ret.at[pl.ds(0, nxc - 1)], rx_r)

    def finish(i, _):
        span = pl.ds(i * tile_t, tile_t)
        flat = pl.ds(pl.multiple_of(i * tile_r, tile_r), tile_r)
        raw = jnp.zeros((tile_r, units), jnp.float32)
        for other in range(nxc):
            raw = raw + lax.dot_general(
                pick[flat, other * wide : (other + 1) * wide], ret[other], NT,
                preferred_element_type=jnp.float32,
            )
        g = gate[span].astype(jnp.float32).reshape(tile_r, units)
        u = up[span].astype(jnp.float32).reshape(tile_r, units)
        s = 1.0 / (1.0 + jnp.exp(-g))
        silu = g * s
        scaled = combine_c[flat] * raw
        gate_out[span] = (scaled * u * s * (1.0 + g * (1.0 - s))).astype(jnp.bfloat16).reshape(
            tile_t, top, units
        )
        up_out[span] = (scaled * silu).astype(jnp.bfloat16).reshape(tile_t, top, units)
        sums = lax.dot_general(
            jnp.ones((8, units), jnp.float32), silu * u * raw, NT,
            precision=lax.Precision.HIGHEST, preferred_element_type=jnp.float32,
        )
        cgp[pl.ds(i, 1), :] = sums[0:1, :]
        return 0

    lax.fori_loop(0, tiles, finish, 0)
    for e in range(1, ntp):
        remote(cgp, cgr.at[y], cg_s, cg_r, at_y((y + e) % ntp)).start()
    cgr[y] = cgp[...]
    drain(cgr.at[pl.ds(0, ntp - 1)], cg_r)
    summed = cgr[0]
    for q in range(1, ntp):
        summed = summed + cgr[q]
    cg_out[...] = summed

    for direction in range(2):
        for step in range(half_z):
            for part in range(2):
                if step < half_z - 1 or part == direction:
                    ring(grad, z, direction, step, part).wait_send()
            if step < half_z - 1 or direction == 0:
                ring_slots(sbuf.at[z], z, direction, step).wait_send()

    def settle(d, _):
        source = (z + d) % nz
        drain(xs.at[source, pl.ds(0, block - cap)], xs_s.at[source])
        drain(hs.at[source], rs_s.at[source])

        @pl.when(d > 0)
        def _():
            drain(zsend.at[source], zr_s.at[source])
            drain(wz.at[source], wz_s.at[source])

        return 0

    lax.fori_loop(0, nz, settle, 0)
    drain(wx.at[pl.ds(0, nxc - 1)], wx_s)
    drain(wt.at[pl.ds(0, ntp - 1)], wy_s)
    drain(xsend.at[pl.ds(0, nxc - 1)], rx_s)
    drain(cgr.at[pl.ds(0, ntp - 1)], cg_s)


def body(nz, nxc, grad_out, routes, combine, gate_act, up_act, w_down):
    tokens, top = routes.shape
    feats = grad_out.shape[1]
    units = gate_act.shape[2]
    ntp = lax.axis_size("tp")
    cap = 2 * tokens * top // (nz * nxc)
    block, wide, experts = nxc * cap, nz * cap, nz * nxc
    tile_t = min(16, tokens)
    half_z = nz // 2
    bf16, f32, i32 = jnp.bfloat16, jnp.float32, jnp.int32
    dma = pltpu.SemaphoreType.DMA
    vmem = pl.BlockSpec(memory_space=pltpu.VMEM)
    scratch = [
        pltpu.VMEM((nz, tokens, feats), bf16),
        pltpu.VMEM((nz, top, tokens), i32),
        pltpu.VMEM((nz, block, feats), bf16),
        pltpu.VMEM((nz, block, feats), bf16),
        pltpu.VMEM((nz, ntp - 1, units, block), bf16),
        pltpu.VMEM((nz, ntp, units, block), bf16),
        pltpu.VMEM((nz, units, block), bf16),
        pltpu.VMEM((nz, units, block), bf16),
        pltpu.VMEM((nxc, units, wide), bf16),
        pltpu.VMEM((nxc, units, wide), bf16),
        pltpu.VMEM((nz, units, block), bf16),
        pltpu.VMEM((ntp, units, nz * block), bf16),
        pltpu.VMEM((nxc, units, wide), bf16),
        pltpu.VMEM((nxc, units, wide), bf16),
        pltpu.VMEM((tokens * top, nxc * wide), bf16),
        pltpu.VMEM((units, tokens * top), bf16),
        pltpu.VMEM((tokens, experts), f32),
        pltpu.VMEM((tokens // tile_t, tile_t * top), f32),
        pltpu.VMEM((ntp, tokens // tile_t, tile_t * top), f32),
        dma((2, half_z, 2)), dma((2, half_z, 2)), dma((2, half_z)), dma((2, half_z)),
        dma((nz,)), dma((nz,)), dma((nz,)), dma((nz,)), dma((nz,)), dma((nz,)),
        dma(()), dma(()), dma((nz,)), dma((nz,)), dma(()), dma(()),
        dma(()), dma(()), dma(()), dma(()),
    ]
    w_grad, gate_grad, up_grad, combine_grad = pl.pallas_call(
        functools.partial(kernel, nz, nxc, ntp, cap),
        out_shape=(
            jax.ShapeDtypeStruct(w_down.shape, bf16),
            jax.ShapeDtypeStruct(gate_act.shape, bf16),
            jax.ShapeDtypeStruct(up_act.shape, bf16),
            jax.ShapeDtypeStruct((tokens // tile_t, tile_t * top), f32),
        ),
        in_specs=[vmem] * 7,
        out_specs=(vmem,) * 4,
        scratch_shapes=scratch,
        compiler_params=pltpu.CompilerParams(
            collective_id=0, has_side_effects=True, vmem_limit_bytes=56 * 1024 * 1024
        ),
    )(
        grad_out, routes.T, routes.reshape(-1, 1), combine.reshape(-1, 1), gate_act, up_act,
        w_down,
    )
    return w_grad, gate_grad, up_grad, combine_grad.reshape(tokens, top)


def solution(mesh, nz=16):
    placed = (
        P("ep", "tp"),
        P("ep", None),
        P("ep", None),
        P("ep", None, "tp"),
        P("ep", None, "tp"),
        P("ep", None, "tp"),
    )
    return jax.shard_map(
        functools.partial(body, nz, mesh.shape["ep"] // nz),
        mesh=mesh,
        in_specs=placed,
        out_specs=(P("ep", None, "tp"), P("ep", None, "tp"), P("ep", None, "tp"), P("ep", None)),
        check_vma=False,
    )
```

```python
import functools

import jax
import jax.numpy as jnp
from jax import lax
from jax.experimental import pallas as pl
from jax.experimental.pallas import tpu as pltpu
from jax.sharding import PartitionSpec as P

MESH = pl.DeviceIdType.MESH
NT = (((1,), (1,)), ((), ()))


def regroup(blocks, cap):
    count = len(blocks)
    lane = lax.broadcasted_iota(jnp.int32, blocks[0].shape, 1)
    lanes = blocks[0].shape[1]
    bit = 1
    while bit < count:
        high = (lane & (bit * cap)) != 0
        fresh = list(blocks)
        for low in range(count):
            if low & bit:
                continue
            a, b = blocks[low], blocks[low | bit]
            fresh[low] = jnp.where(high, pltpu.roll(b, bit * cap, 1), a)
            fresh[low | bit] = jnp.where(high, b, pltpu.roll(a, lanes - bit * cap, 1))
        blocks = fresh
        bit *= 2
    return blocks


def kernel(
    nz, nxc, ntp, cap, plan,
    grad, routes, combine, gate_in, up_in, w_in,
    wgrad_out, gate_out, up_out, cg_out,
    gate, up, w, wgrad, rank,
    zbuf, sbuf, xs, rows, hs, rs, zsend, zret, wx, wxr, wz, wt, xsend, ret, pick, wtok, fa, fb, fh,
    acc, cgp, cgr,
    zg_s, zg_r, sl_s, sl_r, xs_s, xs_r, rs_s, rs_r, zr_s, zr_r, wx_s, wx_r, wz_s, wz_r, wy_s, wy_r,
    rx_s, rx_r, cg_s, cg_r, in_s, out_s,
):
    lag_project, lag_give, weigh_at, place_at, regroup_at, spread_each = plan
    tokens, feats = grad.shape
    top, units = gate.shape[0], gate.shape[1]
    experts = nz * nxc
    block = nxc * cap
    groups = nz // nxc
    wide = nxc * block
    near = nxc // 2
    half_z = nz // 2
    half_t = tokens // 2

    ep, y = lax.axis_index("ep"), lax.axis_index("tp")
    z, xc = ep // nxc, ep % nxc

    def at_z(other):
        return (other * nxc + xc, y)

    def at_xc(other):
        return (z * nxc + other, y)

    def at_y(other):
        return (ep, other)

    def remote(src, dst, send, recv, device):
        return pltpu.make_async_remote_copy(
            src_ref=src, dst_ref=dst, send_sem=send, recv_sem=recv, device_id=device,
            device_id_type=MESH,
        )

    def drain(ref, sem):
        pltpu.make_async_copy(ref, ref, sem).wait()

    def lanes_of(index):
        return pl.ds(pl.multiple_of(index * block, block), block)

    def rows_of(index):
        return pl.ds(pl.multiple_of(index * cap, cap), cap)

    loads = [
        pltpu.make_async_copy(source, target, in_s.at[i])
        for i, (source, target) in enumerate(((gate_in, gate), (up_in, up), (w_in, w)))
    ]
    for load in loads:
        load.start()

    barrier = pltpu.get_barrier_semaphore()

    def greet(count, me, place):
        def one(d, _):
            pl.semaphore_signal(
                barrier, inc=1, device_id=place((me + d) % count), device_id_type=MESH
            )
            return 0

        lax.fori_loop(1, count, one, 0)

    greet(nz, z, at_z)
    greet(nxc, xc, at_xc)
    greet(ntp, y, at_y)
    pl.semaphore_wait(barrier, nz + nxc + ntp - 3)

    ahead = ((z + 1) % nz, (z + nz - 1) % nz)

    def ring(src, source, direction, step, part):
        span = pl.ds(part * half_t, half_t)
        return remote(
            src.at[span], zbuf.at[source, span], zg_s.at[direction, step, part],
            zg_r.at[direction, step, part], at_z(ahead[direction]),
        )

    def ring_slots(src, source, direction, step):
        return remote(
            src, sbuf.at[source], sl_s.at[direction, step], sl_r.at[direction, step],
            at_z(ahead[direction]),
        )

    for part in range(2):
        for direction in range(2):
            ring(grad, z, direction, 0, part).start()

    expert_of = lax.broadcasted_iota(jnp.int32, (experts, tokens), 0)
    named = jnp.zeros((experts, tokens), jnp.float32)
    for k in range(top):
        named = named + jnp.where(routes[k : k + 1, :] == expert_of, 1.0, 0.0)
    before = lax.broadcasted_iota(jnp.int32, (tokens, tokens), 0) < lax.broadcasted_iota(
        jnp.int32, (tokens, tokens), 1
    )
    rank[...] = jnp.dot(
        named.astype(jnp.bfloat16),
        jnp.where(before, 1.0, 0.0).astype(jnp.bfloat16),
        preferred_element_type=jnp.float32,
    )
    code = rank[...] + (expert_of * cap).astype(jnp.float32)
    for k in range(top):
        picked = jnp.where(routes[k : k + 1, :] == expert_of, code, 0.0)
        sbuf[z, k : k + 1, :] = jnp.sum(picked, axis=0, keepdims=True).astype(jnp.int32)
    for direction in range(2):
        ring_slots(sbuf.at[z], z, direction, 0).start()

    def deal(source, chunk):
        at = lax.broadcasted_iota(jnp.int32, (block, tokens), 0) + z * block
        chosen = sbuf[source, 0:1, :] == at
        for k in range(1, top):
            chosen = chosen | (sbuf[source, k : k + 1, :] == at)
        select = jnp.where(chosen, 1.0, 0.0).astype(jnp.bfloat16)
        piece = min(256, feats)
        for lo in range(0, feats, piece):
            xs[source, :, lo : lo + piece] = jnp.dot(
                select, chunk[:, lo : lo + piece], preferred_element_type=jnp.float32
            ).astype(jnp.bfloat16)
        rows[source, rows_of(xc), :] = xs[source, rows_of(xc), :]

        def send(d, _):
            other = (xc + d) % nxc
            remote(
                xs.at[source, rows_of(other)], rows.at[source, rows_of(xc)],
                xs_s.at[source], xs_r.at[source], at_xc(other),
            ).start()
            return 0

        lax.fori_loop(1, nxc, send, 0)

    deal(z, grad)
    loads[2].wait()

    def weigh():
        loads[0].wait()
        loads[1].wait()
        away = (expert_of // nxc - z + near + nz) % nz
        base = (away // nxc) * wide + (expert_of % nxc) * block + (away % nxc) * cap
        code = rank[...] + base.astype(jnp.float32)
        for k in range(top):
            picked = jnp.where(routes[k : k + 1, :] == expert_of, code, 0.0)
            slot = jnp.sum(picked, axis=0, keepdims=True).astype(jnp.int32)
            lanes = slice(k * tokens, (k + 1) * tokens)

            def mark(i, _):
                span = pl.ds(pl.multiple_of(i * block, block), block)
                at = lax.broadcasted_iota(jnp.int32, (block, tokens), 0) + i * block
                pick[span, lanes] = jnp.where(slot == at, 1.0, 0.0).astype(jnp.bfloat16)
                return 0

            lax.fori_loop(0, nz, mark, 0)

            g = gate[k].astype(jnp.float32)
            u = up[k].astype(jnp.float32)
            c = combine[k : k + 1, :]
            s = 1.0 / (1.0 + jnp.exp(-g))
            silu = g * s
            hidden = silu * u
            fh[k] = hidden
            fa[k] = c * u * s * (1.0 + g * (1.0 - s))
            fb[k] = c * silu
            wtok[:, lanes] = (c * hidden).astype(jnp.bfloat16)

    def place_weighted(i, _):
        part, pair = i // (nxc // 2), i % (nxc // 2)
        span = pl.ds(pl.multiple_of(i * 2 * block, 2 * block), 2 * block)
        value = lax.dot_general(
            wtok[...], pick[span, :], NT, preferred_element_type=jnp.float32
        ).astype(jnp.bfloat16)
        wx[2 * pair, part] = value[:, :block]
        wx[2 * pair + 1, part] = value[:, block:]
        return 0

    def place():
        lax.fori_loop(0, groups * nxc // 2, place_weighted, 0)

        def send_wx(d, _):
            other = (xc + d) % nxc
            remote(wx.at[other], wxr.at[xc], wx_s, wx_r, at_xc(other)).start()
            return 0

        lax.fori_loop(1, nxc, send_wx, 0)
        wxr[xc] = wx[xc]

    strip = 16 if units % 16 == 0 else units

    def order(i):
        return (nz + jnp.where(i % 2 == 1, (i + 1) // 2, -(i // 2))) % nz

    def regroup_weighted():
        drain(wxr.at[pl.ds(0, nxc - 1)], wx_r)

        def one(i, _):
            span = pl.ds(pl.multiple_of(i * strip, strip), strip)
            for part in range(groups):
                blocks = [wxr[o, part, span, :].astype(jnp.float32) for o in range(nxc)]
                for low, value in enumerate(regroup(blocks, cap)):
                    wz[part * nxc + low, span, :] = value.astype(jnp.bfloat16)
            return 0

        lax.fori_loop(0, units // strip, one, 0)

    def send_weighted():
        def send(i, _):
            d = order(i)
            other = (z + d) % nz
            remote(
                wz.at[(d + near) % nz], wt.at[y, :, lanes_of(z)], wz_s.at[other], wz_r.at[z],
                at_z(other),
            ).start()
            return 0

        lax.fori_loop(1, nz, send, 0)
        wt[y, :, lanes_of(z)] = wz[near]

    def spread_weighted(i, _):
        source = (z + nz - order(i)) % nz

        @pl.when(i > 0)
        def _():
            drain(wt.at[y, :, lanes_of(source)], wz_r.at[source])

        for e in range(1, ntp):
            remote(
                wt.at[y, :, lanes_of(source)], wt.at[y, :, lanes_of(source)], wy_s, wy_r,
                at_y((y + e) % ntp),
            ).start()
        return 0

    def project(source):
        drain(rows.at[source, pl.ds(0, block - cap)], xs_r.at[source])
        for d in range(ntp):
            other = (y + ntp - 1 - d) % ntp
            weights = w[0, pl.ds(pl.multiple_of(other * units, units), units), :]
            value = lax.dot_general(
                weights, rows[source], NT, preferred_element_type=jnp.float32
            ).astype(jnp.bfloat16)
            if d == ntp - 1:
                rs[source, y] = value
            else:
                hs[source, d] = value
                remote(
                    hs.at[source, d], rs.at[source, y], rs_s.at[source], rs_r.at[source],
                    at_y(other),
                ).start()

    def total(source):
        drain(rs.at[source, pl.ds(0, ntp - 1)], rs_r.at[source])
        out = rs[source, 0].astype(jnp.float32)
        for q in range(1, ntp):
            out = out + rs[source, q].astype(jnp.float32)
        return out.astype(jnp.bfloat16)

    def give_back(source):
        zsend[source] = total(source)
        away = (z - source + near + nz) % nz
        remote(
            zsend.at[source], zret.at[away], zr_s.at[source], zr_r.at[away], at_z(source)
        ).start()

    def below(step):
        return (z + nz - step) % nz

    def above(step):
        return (z + step) % nz

    def both(step, act):
        act(below(step))
        act(above(step))

    def keep_own():
        zret[near] = total(z)

    def at_step(step, lag, own, act):
        @pl.when(step == lag)
        def _():
            own()

        @pl.when(step > lag)
        def _():
            both(step - lag, act)

    def gather_step(step, _):
        sources = (below(step), above(step))
        for part in range(2):
            for direction in range(2):
                source = sources[direction]
                ring(zbuf.at[source], source, direction, step - 1, part).wait_recv()
                if part == direction:
                    ring(zbuf.at[source], source, direction, step, part).start()
                else:

                    @pl.when(step < half_z - 1)
                    def _():
                        ring(zbuf.at[source], source, direction, step, part).start()

        for direction in range(2):
            source = sources[direction]
            ring_slots(sbuf.at[source], source, direction, step - 1).wait_recv()
            if direction == 0:
                ring_slots(sbuf.at[source], source, direction, step).start()
            else:

                @pl.when(step < half_z - 1)
                def _():
                    ring_slots(sbuf.at[source], source, direction, step).start()

        for direction in range(2):
            deal(sources[direction], zbuf.at[sources[direction]])

        at_step(step, lag_project, lambda: project(z), project)
        at_step(step, lag_give, keep_own, give_back)

        for at, act in ((weigh_at, weigh), (place_at, place), (regroup_at, regroup_weighted)):

            @pl.when(step == at)
            def _():
                act()

        return 0

    lax.fori_loop(1, half_z, gather_step, 0)

    far = above(half_z)
    for direction in range(2):
        ring(zbuf.at[far], far, direction, half_z - 1, direction).wait_recv()
    ring_slots(sbuf.at[far], far, 0, half_z - 1).wait_recv()
    if weigh_at >= half_z:
        weigh()
    if place_at >= half_z:
        place()
    if regroup_at >= half_z:
        regroup_weighted()
    send_weighted()
    deal(far, zbuf.at[far])

    def late(step, lag, own, act):
        at = step - lag
        if at == 0:
            own()
        elif 0 < at < half_z:
            both(at, act)
        elif at == half_z:
            act(far)

    spread = 0
    for step in range(half_z, half_z + lag_give + 1):
        late(step, lag_project, lambda: project(z), project)
        late(step, lag_give, keep_own, give_back)
        upto = min(nz, spread + spread_each)
        lax.fori_loop(spread, upto, spread_weighted, 0)
        spread = upto
    lax.fori_loop(spread, nz, spread_weighted, 0)

    def pass_back(part):
        for low in range(nxc):
            index = part * nxc + low
            if index != near:
                drain(zret.at[index], zr_r.at[index])

        def one(i, _):
            span = pl.ds(pl.multiple_of(i * strip, strip), strip)
            blocks = [
                zret[part * nxc + low, span, :].astype(jnp.float32) for low in range(nxc)
            ]
            for other, value in enumerate(regroup(blocks, cap)):
                xsend[part, other, span, :] = value.astype(jnp.bfloat16)
            return 0

        lax.fori_loop(0, units // strip, one, 0)

        def send(d, _):
            other = (xc + d) % nxc
            remote(
                xsend.at[part, other], ret.at[part, :, lanes_of(xc)], rx_s.at[part],
                rx_r.at[part], at_xc(other),
            ).start()
            return 0

        lax.fori_loop(1, nxc, send, 0)
        ret[part, :, lanes_of(xc)] = xsend[part, xc]

    for part in range(groups - 1):
        pass_back(part)

    drain(wt.at[pl.ds(0, ntp - 1)], wy_r)
    piece = min(256, feats)
    per = feats // piece

    def weight_gradient(i, _):
        q, n = i // per, i % per
        cols = pl.ds(pl.multiple_of(n * piece, piece), piece)
        wgrad[0, pl.ds(pl.multiple_of(q * units, units), units), cols] = jnp.dot(
            wt[q],
            rows[:, :, cols].reshape(nz * block, piece),
            preferred_element_type=jnp.float32,
        ).astype(jnp.bfloat16)
        return 0

    lax.fori_loop(0, ntp * per, weight_gradient, 0)
    store = pltpu.make_async_copy(wgrad, wgrad_out, out_s)
    store.start()

    pair = min(2, top) * tokens

    def collect(part):
        drain(ret.at[part, :, pl.ds(0, wide - block)], rx_r.at[part])

        def one(i, _):
            cols = pl.ds(pl.multiple_of(i * pair, pair), pair)
            value = jnp.dot(
                ret[part], pick[part * wide : (part + 1) * wide, cols],
                preferred_element_type=jnp.float32,
            )
            acc[:, cols] = value if part == 0 else acc[:, cols] + value
            return 0

        lax.fori_loop(0, top * tokens // pair, one, 0)

    for part in range(groups - 1):
        collect(part)
    pass_back(groups - 1)
    collect(groups - 1)

    for k in range(top):
        raw = acc[:, k * tokens : (k + 1) * tokens]
        cgp[k : k + 1, :] = jnp.sum(fh[k] * raw, axis=0, keepdims=True)
    for e in range(1, ntp):
        remote(cgp, cgr.at[y], cg_s, cg_r, at_y((y + e) % ntp)).start()
    cgr[y] = cgp[...]
    for k in range(top):
        raw = acc[:, k * tokens : (k + 1) * tokens]
        gate_out[k] = (fa[k] * raw).astype(jnp.bfloat16)
        up_out[k] = (fb[k] * raw).astype(jnp.bfloat16)

    for direction in range(2):
        for step in range(half_z):
            for part in range(2):
                if step < half_z - 1 or part == direction:
                    ring(grad, z, direction, step, part).wait_send()
            if step < half_z - 1 or direction == 0:
                ring_slots(sbuf.at[z], z, direction, step).wait_send()

    def settle(d, _):
        source = (z + d) % nz
        drain(xs.at[source, pl.ds(0, block - cap)], xs_s.at[source])
        drain(hs.at[source], rs_s.at[source])

        @pl.when(d > 0)
        def _():
            drain(zsend.at[source], zr_s.at[source])
            drain(wz.at[source], wz_s.at[source])

        return 0

    lax.fori_loop(0, nz, settle, 0)
    drain(wx.at[pl.ds(0, nxc - 1)], wx_s)
    drain(wt.at[pl.ds(0, ntp - 1)], wy_s)
    for part in range(groups):
        drain(xsend.at[part, pl.ds(0, nxc - 1)], rx_s.at[part])
    drain(cgr.at[pl.ds(0, ntp - 1)], cg_s)
    drain(cgr.at[pl.ds(0, ntp - 1)], cg_r)
    summed = cgr[0]
    for q in range(1, ntp):
        summed = summed + cgr[q]
    cg_out[...] = summed
    store.wait()


PLAN = (3, 4, 1, 2, 6, 4)


def body(nz, nxc, grad_out, routes, combine, gate_act, up_act, w_down):
    tokens, top = routes.shape
    feats = grad_out.shape[1]
    units = gate_act.shape[2]
    ntp = lax.axis_size("tp")
    cap = 2 * tokens * top // (nz * nxc)
    block, groups = nxc * cap, nz // nxc
    half_z = nz // 2
    bf16, f32, i32 = jnp.bfloat16, jnp.float32, jnp.int32
    dma = pltpu.SemaphoreType.DMA
    vmem = pl.BlockSpec(memory_space=pltpu.VMEM)
    anywhere = pl.BlockSpec(memory_space=pl.ANY)
    scratch = [
        pltpu.VMEM((top, units, tokens), bf16),
        pltpu.VMEM((top, units, tokens), bf16),
        pltpu.VMEM(w_down.shape, bf16),
        pltpu.VMEM(w_down.shape, bf16),
        pltpu.VMEM((nz * nxc, tokens), f32),
        pltpu.VMEM((nz, tokens, feats), bf16),
        pltpu.VMEM((nz, top, tokens), i32),
        pltpu.VMEM((nz, block, feats), bf16),
        pltpu.VMEM((nz, block, feats), bf16),
        pltpu.VMEM((nz, ntp - 1, units, block), bf16),
        pltpu.VMEM((nz, ntp, units, block), bf16),
        pltpu.VMEM((nz, units, block), bf16),
        pltpu.VMEM((nz, units, block), bf16),
        pltpu.VMEM((nxc, groups, units, block), bf16),
        pltpu.VMEM((nxc, groups, units, block), bf16),
        pltpu.VMEM((nz, units, block), bf16),
        pltpu.VMEM((ntp, units, nz * block), bf16),
        pltpu.VMEM((groups, nxc, units, block), bf16),
        pltpu.VMEM((groups, units, nxc * block), bf16),
        pltpu.VMEM((nz * block, top * tokens), bf16),
        pltpu.VMEM((units, top * tokens), bf16),
        pltpu.VMEM((top, units, tokens), f32),
        pltpu.VMEM((top, units, tokens), f32),
        pltpu.VMEM((top, units, tokens), f32),
        pltpu.VMEM((units, top * tokens), f32),
        pltpu.VMEM((top, tokens), f32),
        pltpu.VMEM((ntp, top, tokens), f32),
        dma((2, half_z, 2)), dma((2, half_z, 2)), dma((2, half_z)), dma((2, half_z)),
        dma((nz,)), dma((nz,)), dma((nz,)), dma((nz,)), dma((nz,)), dma((nz,)),
        dma(()), dma(()), dma((nz,)), dma((nz,)), dma(()), dma(()),
        dma((groups,)), dma((groups,)), dma(()), dma(()), dma((3,)), dma(()),
    ]
    w_grad, gate_grad, up_grad, combine_grad = pl.pallas_call(
        functools.partial(kernel, nz, nxc, ntp, cap, PLAN),
        out_shape=(
            jax.ShapeDtypeStruct(w_down.shape, bf16),
            jax.ShapeDtypeStruct((top, units, tokens), bf16),
            jax.ShapeDtypeStruct((top, units, tokens), bf16),
            jax.ShapeDtypeStruct((top, tokens), f32),
        ),
        in_specs=[vmem] * 3 + [anywhere] * 3,
        out_specs=(anywhere,) + (vmem,) * 3,
        scratch_shapes=scratch,
        compiler_params=pltpu.CompilerParams(
            collective_id=0, has_side_effects=True, vmem_limit_bytes=56 * 1024 * 1024
        ),
    )(
        grad_out, routes.T, combine.T, jnp.transpose(gate_act, (1, 2, 0)),
        jnp.transpose(up_act, (1, 2, 0)), w_down,
    )
    return (
        w_grad,
        jnp.transpose(gate_grad, (2, 0, 1)),
        jnp.transpose(up_grad, (2, 0, 1)),
        combine_grad.T,
    )


def solution(mesh, nz=16):
    placed = (
        P("ep", "tp"),
        P("ep", None),
        P("ep", None),
        P("ep", None, "tp"),
        P("ep", None, "tp"),
        P("ep", None, "tp"),
    )
    return jax.shard_map(
        functools.partial(body, nz, mesh.shape["ep"] // nz),
        mesh=mesh,
        in_specs=placed,
        out_specs=(P("ep", None, "tp"), P("ep", None, "tp"), P("ep", None, "tp"), P("ep", None)),
        check_vma=False,
    )
```

```python
import functools

import jax
import jax.numpy as jnp
from jax import lax
from jax.experimental import pallas as pl
from jax.experimental.pallas import tpu as pltpu
from jax.sharding import PartitionSpec as P

MESH = pl.DeviceIdType.MESH
NT = (((1,), (1,)), ((), ()))


def regroup(blocks, cap):
    count = len(blocks)
    lane = lax.broadcasted_iota(jnp.int32, blocks[0].shape, 1)
    lanes = blocks[0].shape[1]
    bit = 1
    while bit < count:
        high = (lane & (bit * cap)) != 0
        fresh = list(blocks)
        for low in range(count):
            if low & bit:
                continue
            a, b = blocks[low], blocks[low | bit]
            fresh[low] = jnp.where(high, pltpu.roll(b, bit * cap, 1), a)
            fresh[low | bit] = jnp.where(high, b, pltpu.roll(a, lanes - bit * cap, 1))
        blocks = fresh
        bit *= 2
    return blocks


def kernel(
    nz, nxc, ntp, cap, plan,
    grad, routes, combine, gate_in, up_in, w_in,
    wgrad_out, act_out, cg_out,
    gate, up, w, wgrad, rank,
    zbuf, sbuf, xs, rows, hs, rs, summed, xsend, xret, zsend, ret, wx, wxr, wz, wt, pick, wtok,
    fa, fb, fh, acc, gate_grad, up_grad, cgp, cgr,
    zg_s, zg_r, sl_s, sl_r, xs_s, xs_r, rs_s, rs_r, zr_s, zr_r, wx_s, wx_r, wz_s, wz_r, wy_s, wy_r,
    rx_s, rx_r, cg_s, cg_r, in_s, out_s,
):
    lag_project, lag_give, regroup_at, spread_each = plan
    tokens, feats = grad.shape
    top, units = gate.shape[0], gate.shape[1]
    experts = nz * nxc
    block = nxc * cap
    groups = nz // nxc
    wide = nxc * block
    near = nxc // 2
    half_z = nz // 2
    half_t = tokens // 2

    ep, y = lax.axis_index("ep"), lax.axis_index("tp")
    z, xc = ep // nxc, ep % nxc

    def at_z(other):
        return (other * nxc + xc, y)

    def at_xc(other):
        return (z * nxc + other, y)

    def at_y(other):
        return (ep, other)

    def remote(src, dst, send, recv, device):
        return pltpu.make_async_remote_copy(
            src_ref=src, dst_ref=dst, send_sem=send, recv_sem=recv, device_id=device,
            device_id_type=MESH,
        )

    def drain(ref, sem):
        pltpu.make_async_copy(ref, ref, sem).wait()

    def lanes_of(index):
        return pl.ds(pl.multiple_of(index * block, block), block)

    def rows_of(index):
        return pl.ds(pl.multiple_of(index * cap, cap), cap)

    def order(i, count=nz):
        return (count + jnp.where(i % 2 == 1, (i + 1) // 2, -(i // 2))) % count

    loads = [
        pltpu.make_async_copy(source, target, in_s.at[i])
        for i, (source, target) in enumerate(((gate_in, gate), (up_in, up), (w_in, w)))
    ]
    for load in loads:
        load.start()

    barrier = pltpu.get_barrier_semaphore()

    def greet(count, me, place):
        def one(i, _):
            d = order(i, count)
            pl.semaphore_signal(
                barrier, inc=1, device_id=place((me + d) % count), device_id_type=MESH
            )
            return 0

        lax.fori_loop(1, count, one, 0)

    greet(nz, z, at_z)
    greet(nxc, xc, at_xc)
    greet(ntp, y, at_y)
    pl.semaphore_wait(barrier, nz + nxc + ntp - 3)

    ahead = ((z + 1) % nz, (z + nz - 1) % nz)

    def ring(src, source, direction, step, part):
        span = pl.ds(part * half_t, half_t)
        return remote(
            src.at[span], zbuf.at[source, span], zg_s.at[direction, step, part],
            zg_r.at[direction, step, part], at_z(ahead[direction]),
        )

    def ring_slots(src, source, direction, step):
        return remote(
            src, sbuf.at[source], sl_s.at[direction, step], sl_r.at[direction, step],
            at_z(ahead[direction]),
        )

    for part in range(2):
        for direction in range(2):
            ring(grad, z, direction, 0, part).start()

    expert_of = lax.broadcasted_iota(jnp.int32, (experts, tokens), 0)
    named = jnp.zeros((experts, tokens), jnp.float32)
    for k in range(top):
        named = named + jnp.where(routes[k : k + 1, :] == expert_of, 1.0, 0.0)
    before = lax.broadcasted_iota(jnp.int32, (tokens, tokens), 0) < lax.broadcasted_iota(
        jnp.int32, (tokens, tokens), 1
    )
    rank[...] = jnp.dot(
        named.astype(jnp.bfloat16),
        jnp.where(before, 1.0, 0.0).astype(jnp.bfloat16),
        preferred_element_type=jnp.float32,
    )
    code = rank[...] + (expert_of * cap).astype(jnp.float32)
    for k in range(top):
        picked = jnp.where(routes[k : k + 1, :] == expert_of, code, 0.0)
        sbuf[z, k : k + 1, :] = jnp.sum(picked, axis=0, keepdims=True).astype(jnp.int32)
    for direction in range(2):
        ring_slots(sbuf.at[z], z, direction, 0).start()

    def deal(source, chunk):
        at = lax.broadcasted_iota(jnp.int32, (block, tokens), 0) + z * block
        chosen = sbuf[source, 0:1, :] == at
        for k in range(1, top):
            chosen = chosen | (sbuf[source, k : k + 1, :] == at)
        select = jnp.where(chosen, 1.0, 0.0).astype(jnp.bfloat16)
        piece = min(256, feats)
        for lo in range(0, feats, piece):
            xs[source, :, lo : lo + piece] = jnp.dot(
                select, chunk[:, lo : lo + piece], preferred_element_type=jnp.float32
            ).astype(jnp.bfloat16)
        rows[source, rows_of(xc), :] = xs[source, rows_of(xc), :]

        def send(d, _):
            other = (xc + d) % nxc
            remote(
                xs.at[source, rows_of(other)], rows.at[source, rows_of(xc)],
                xs_s.at[source], xs_r.at[source], at_xc(other),
            ).start()
            return 0

        lax.fori_loop(1, nxc, send, 0)

    deal(z, grad)
    loads[2].wait()

    def weigh(lower, upper):
        if lower == 0:
            loads[0].wait()
            loads[1].wait()
        away = (z - expert_of // nxc + near + nz) % nz
        base = away * block + (expert_of % nxc) * cap
        code = rank[...] + base.astype(jnp.float32)
        for k in range(lower, upper):
            picked = jnp.where(routes[k : k + 1, :] == expert_of, code, 0.0)
            slot = jnp.sum(picked, axis=0, keepdims=True).astype(jnp.int32)
            lanes = slice(k * tokens, (k + 1) * tokens)

            def mark(i, _):
                span = pl.ds(pl.multiple_of(i * block, block), block)
                at = lax.broadcasted_iota(jnp.int32, (block, tokens), 0) + i * block
                pick[span, lanes] = jnp.where(slot == at, 1.0, 0.0).astype(jnp.bfloat16)
                return 0

            lax.fori_loop(0, nz, mark, 0)

            g = gate[k].astype(jnp.float32)
            u = up[k].astype(jnp.float32)
            c = combine[k : k + 1, :]
            s = 1.0 / (1.0 + jnp.exp(-g))
            silu = g * s
            hidden = silu * u
            fh[k] = hidden
            fa[k] = c * u * s * (1.0 + g * (1.0 - s))
            fb[k] = c * silu
            wtok[:, lanes] = (c * hidden).astype(jnp.bfloat16)

    def place_weighted(i, _):
        part, pair = i // (nxc // 2), i % (nxc // 2)
        slots = [
            pick[rows_of((part * nxc + low) * nxc + 2 * pair + side), :]
            for side in range(2)
            for low in range(nxc)
        ]
        value = lax.dot_general(
            wtok[...], jnp.concatenate(slots, axis=0), NT, preferred_element_type=jnp.float32
        ).astype(jnp.bfloat16)
        wx[2 * pair, part] = value[:, :block]
        wx[2 * pair + 1, part] = value[:, block:]
        return 0

    def place(lower, upper):
        lax.fori_loop(lower * nxc // 2, upper * nxc // 2, place_weighted, 0)
        if upper < groups:
            return

        def send_wx(d, _):
            other = (xc + d) % nxc
            remote(wx.at[other], wxr.at[xc], wx_s, wx_r, at_xc(other)).start()
            return 0

        lax.fori_loop(1, nxc, send_wx, 0)
        wxr[xc] = wx[xc]

    strip = 16 if units % 16 == 0 else units

    def regroup_weighted():
        drain(wxr.at[pl.ds(0, nxc - 1)], wx_r)

        def one(i, _):
            span = pl.ds(pl.multiple_of(i * strip, strip), strip)
            for part in range(groups):
                blocks = [wxr[o, part, span, :].astype(jnp.float32) for o in range(nxc)]
                for low, value in enumerate(regroup(blocks, cap)):
                    wz[part * nxc + low, span, :] = value.astype(jnp.bfloat16)
            return 0

        lax.fori_loop(0, units // strip, one, 0)

    def send_weighted():
        def send(i, _):
            d = order(i)
            other = (z + d) % nz
            remote(
                wz.at[(near + nz - d) % nz], wt.at[y, :, lanes_of(z)], wz_s.at[other], wz_r.at[z],
                at_z(other),
            ).start()
            return 0

        lax.fori_loop(1, nz, send, 0)
        wt[y, :, lanes_of(z)] = wz[near]

    def spread_weighted(i, _):
        source = (z + nz - order(i)) % nz

        @pl.when(i > 0)
        def _():
            drain(wt.at[y, :, lanes_of(source)], wz_r.at[source])

        for e in range(1, ntp):
            remote(
                wt.at[y, :, lanes_of(source)], wt.at[y, :, lanes_of(source)], wy_s, wy_r,
                at_y((y + e) % ntp),
            ).start()
        return 0

    def project(source):
        drain(rows.at[source, pl.ds(0, block - cap)], xs_r.at[source])
        for d in range(ntp):
            other = (y + ntp - 1 - d) % ntp
            weights = w[0, pl.ds(pl.multiple_of(other * units, units), units), :]
            value = lax.dot_general(
                weights, rows[source], NT, preferred_element_type=jnp.float32
            ).astype(jnp.bfloat16)
            if d == ntp - 1:
                rs[source, y] = value
            else:
                hs[source, d] = value
                remote(
                    hs.at[source, d], rs.at[source, y], rs_s.at[source], rs_r.at[source],
                    at_y(other),
                ).start()

    def total(source):
        drain(rs.at[source, pl.ds(0, ntp - 1)], rs_r.at[source])
        out = rs[source, 0].astype(jnp.float32)
        for q in range(1, ntp):
            out = out + rs[source, q].astype(jnp.float32)
        return out.astype(jnp.bfloat16)

    def add_up(source):
        summed[(source - z + near + nz) % nz] = total(source)

    def regroup_group(part, take, put):
        def one(i, _):
            span = pl.ds(pl.multiple_of(i * strip, strip), strip)
            blocks = [take(low, span).astype(jnp.float32) for low in range(nxc)]
            for other, value in enumerate(regroup(blocks, cap)):
                put(other, span, value.astype(jnp.bfloat16))
            return 0

        lax.fori_loop(0, units // strip, one, 0)

    def return_x(part):
        def put(other, span, value):
            xsend[part, other, span, :] = value

        regroup_group(part, lambda low, span: summed[part * nxc + low, span, :], put)

        def send(d, _):
            other = (xc + d) % nxc
            remote(
                xsend.at[part, other], xret.at[part, xc], rx_s.at[part], rx_r.at[part],
                at_xc(other),
            ).start()
            return 0

        lax.fori_loop(1, nxc, send, 0)
        xret[part, xc] = xsend[part, xc]

    def return_z(part):
        drain(xret.at[part, pl.ds(0, nxc - 1)], rx_r.at[part])

        def put(low, span, value):
            zsend[part * nxc + low, span, :] = value

        regroup_group(part, lambda other, span: xret[part, other, span, :], put)
        for low in range(nxc):
            index = part * nxc + low
            lanes = slice(low * block, (low + 1) * block)
            if index == near:
                ret[part, :, lanes] = zsend[index]
            else:
                remote(
                    zsend.at[index], ret.at[part, :, pl.ds(low * block, block)],
                    zr_s.at[index], zr_r.at[index], at_z((z + index - near + nz) % nz),
                ).start()

    def below(step):
        return (z + nz - step) % nz

    def above(step):
        return (z + step) % nz

    def both(step, act):
        act(below(step))
        act(above(step))

    def at_step(step, lag, own, act):
        @pl.when(step == lag)
        def _():
            own()

        @pl.when(step > lag)
        def _():
            both(step - lag, act)

    share = -(-top // 3)
    middle = groups // 2
    work = [
        (1, lambda: weigh(0, share)),
        (2, lambda: weigh(share, 2 * share)),
        (3, lambda: weigh(2 * share, top)),
        (half_z - 4, lambda: place(0, middle)),
        (half_z - 3, lambda: place(middle, groups)),
        (regroup_at, regroup_weighted),
    ]

    def gather_step(step, _):
        sources = (below(step), above(step))
        for part in range(2):
            for direction in range(2):
                source = sources[direction]
                ring(zbuf.at[source], source, direction, step - 1, part).wait_recv()
                if part == direction:
                    ring(zbuf.at[source], source, direction, step, part).start()
                else:

                    @pl.when(step < half_z - 1)
                    def _():
                        ring(zbuf.at[source], source, direction, step, part).start()

        for direction in range(2):
            source = sources[direction]
            ring_slots(sbuf.at[source], source, direction, step - 1).wait_recv()
            if direction == 0:
                ring_slots(sbuf.at[source], source, direction, step).start()
            else:

                @pl.when(step < half_z - 1)
                def _():
                    ring_slots(sbuf.at[source], source, direction, step).start()

        for direction in range(2):
            deal(sources[direction], zbuf.at[sources[direction]])

        at_step(step, lag_project, lambda: project(z), project)
        at_step(step, lag_give, lambda: add_up(z), add_up)

        for at, act in work:

            @pl.when(step == at)
            def _():
                act()

        return 0

    lax.fori_loop(1, half_z, gather_step, 0)

    def late(step, lag, own, act):
        at = step - lag
        if at == 0:
            own()
        elif 0 < at < half_z:
            both(at, act)
        elif at == half_z:
            act(far)

    def spread(count):
        upto = min(nz, spread_to[-1] + count)
        lax.fori_loop(spread_to[-1], upto, spread_weighted, 0)
        spread_to.append(upto)

    spread_to = [0]
    early = lag_give + near < half_z
    if regroup_at >= half_z:
        regroup_weighted()
    send_weighted()
    if early:
        return_x(0)

    far = above(half_z)
    for direction in range(2):
        ring(zbuf.at[far], far, direction, half_z - 1, direction).wait_recv()
    ring_slots(sbuf.at[far], far, 0, half_z - 1).wait_recv()
    deal(far, zbuf.at[far])

    for step in range(half_z, half_z + lag_give + 1):
        late(step, lag_project, lambda: project(z), project)
        late(step, lag_give, lambda: add_up(z), add_up)
        if step == half_z + (0 if early else lag_give):
            if not early:
                return_x(0)
            return_z(0)
        spread(spread_each[min(step - half_z, len(spread_each) - 2)])
    for part in range(1, groups):
        return_x(part)
    spread(spread_each[-1])
    for part in range(1, groups):
        return_z(part)
    spread(nz)

    drain(wt.at[pl.ds(0, ntp - 1)], wy_r)
    piece = min(256, feats)
    per = feats // piece

    def weight_gradient(i, _):
        q, n = i // per, i % per
        cols = pl.ds(pl.multiple_of(n * piece, piece), piece)
        wgrad[0, pl.ds(pl.multiple_of(q * units, units), units), cols] = jnp.dot(
            wt[q],
            rows[:, :, cols].reshape(nz * block, piece),
            preferred_element_type=jnp.float32,
        ).astype(jnp.bfloat16)
        return 0

    lax.fori_loop(0, ntp * per, weight_gradient, 0)
    store = pltpu.make_async_copy(wgrad, wgrad_out, out_s.at[0])
    store.start()

    pair = min(2, top) * tokens

    def collect(part):
        for low in range(nxc):
            index = part * nxc + low
            if index != near:
                drain(zsend.at[index], zr_r.at[index])

        def one(i, _):
            cols = pl.ds(pl.multiple_of(i * pair, pair), pair)
            value = jnp.dot(
                ret[part], pick[part * wide : (part + 1) * wide, cols],
                preferred_element_type=jnp.float32,
            )
            acc[:, cols] = value if part == 0 else acc[:, cols] + value
            return 0

        lax.fori_loop(0, top * tokens // pair, one, 0)

    for part in range(groups - 1):
        collect(part)

    for direction in range(2):
        for step in range(half_z):
            for part in range(2):
                if step < half_z - 1 or part == direction:
                    ring(grad, z, direction, step, part).wait_send()
            if step < half_z - 1 or direction == 0:
                ring_slots(sbuf.at[z], z, direction, step).wait_send()

    def settle(d, _):
        source = (z + d) % nz
        drain(xs.at[source, pl.ds(0, block - cap)], xs_s.at[source])
        drain(hs.at[source], rs_s.at[source])

        @pl.when(d > 0)
        def _():
            drain(wz.at[source], wz_s.at[source])

        return 0

    lax.fori_loop(0, nz, settle, 0)
    drain(wx.at[pl.ds(0, nxc - 1)], wx_s)
    drain(wt.at[pl.ds(0, ntp - 1)], wy_s)
    for part in range(groups):
        drain(xsend.at[part, pl.ds(0, nxc - 1)], rx_s.at[part])
    for index in range(nz):
        if index != near:
            drain(zsend.at[index], zr_s.at[index])
    collect(groups - 1)

    for k in range(top):
        raw = acc[:, k * tokens : (k + 1) * tokens]
        cgp[k : k + 1, :] = jnp.sum(fh[k] * raw, axis=0, keepdims=True)
    for e in range(1, ntp):
        remote(cgp, cgr.at[y], cg_s, cg_r, at_y((y + e) % ntp)).start()
    cgr[y] = cgp[...]
    for k in range(top):
        raw = acc[:, k * tokens : (k + 1) * tokens]
        gate_grad[k] = (fa[k] * raw).astype(jnp.bfloat16)
        up_grad[k] = (fb[k] * raw).astype(jnp.bfloat16)
    stores = [
        store,
        pltpu.make_async_copy(gate_grad, act_out.at[0], out_s.at[1]),
        pltpu.make_async_copy(up_grad, act_out.at[1], out_s.at[2]),
    ]
    stores[1].start()
    stores[2].start()
    drain(cgr.at[pl.ds(0, ntp - 1)], cg_s)
    drain(cgr.at[pl.ds(0, ntp - 1)], cg_r)
    router = cgr[0]
    for q in range(1, ntp):
        router = router + cgr[q]
    cg_out[...] = router
    for copy in stores:
        copy.wait()


PLAN = (2, 3, 8, (0, 0, 0, 4, 4))


def body(nz, nxc, grad_out, routes, combine, gate_act, up_act, w_down):
    tokens, top = routes.shape
    feats = grad_out.shape[1]
    units = gate_act.shape[2]
    ntp = lax.axis_size("tp")
    cap = 2 * tokens * top // (nz * nxc)
    block, groups = nxc * cap, nz // nxc
    half_z = nz // 2
    bf16, f32, i32 = jnp.bfloat16, jnp.float32, jnp.int32
    dma = pltpu.SemaphoreType.DMA
    vmem = pl.BlockSpec(memory_space=pltpu.VMEM)
    anywhere = pl.BlockSpec(memory_space=pl.ANY)
    scratch = [
        pltpu.VMEM((top, units, tokens), bf16),
        pltpu.VMEM((top, units, tokens), bf16),
        pltpu.VMEM(w_down.shape, bf16),
        pltpu.VMEM(w_down.shape, bf16),
        pltpu.VMEM((nz * nxc, tokens), f32),
        pltpu.VMEM((nz, tokens, feats), bf16),
        pltpu.VMEM((nz, top, tokens), i32),
        pltpu.VMEM((nz, block, feats), bf16),
        pltpu.VMEM((nz, block, feats), bf16),
        pltpu.VMEM((nz, ntp - 1, units, block), bf16),
        pltpu.VMEM((nz, ntp, units, block), bf16),
        pltpu.VMEM((nz, units, block), bf16),
        pltpu.VMEM((groups, nxc, units, block), bf16),
        pltpu.VMEM((groups, nxc, units, block), bf16),
        pltpu.VMEM((nz, units, block), bf16),
        pltpu.VMEM((groups, units, nxc * block), bf16),
        pltpu.VMEM((nxc, groups, units, block), bf16),
        pltpu.VMEM((nxc, groups, units, block), bf16),
        pltpu.VMEM((nz, units, block), bf16),
        pltpu.VMEM((ntp, units, nz * block), bf16),
        pltpu.VMEM((nz * block, top * tokens), bf16),
        pltpu.VMEM((units, top * tokens), bf16),
        pltpu.VMEM((top, units, tokens), f32),
        pltpu.VMEM((top, units, tokens), f32),
        pltpu.VMEM((top, units, tokens), f32),
        pltpu.VMEM((units, top * tokens), f32),
        pltpu.VMEM((top, units, tokens), bf16),
        pltpu.VMEM((top, units, tokens), bf16),
        pltpu.VMEM((top, tokens), f32),
        pltpu.VMEM((ntp, top, tokens), f32),
        dma((2, half_z, 2)), dma((2, half_z, 2)), dma((2, half_z)), dma((2, half_z)),
        dma((nz,)), dma((nz,)), dma((nz,)), dma((nz,)), dma((nz,)), dma((nz,)),
        dma(()), dma(()), dma((nz,)), dma((nz,)), dma(()), dma(()),
        dma((groups,)), dma((groups,)), dma(()), dma(()), dma((3,)), dma((3,)),
    ]
    w_grad, act_grad, combine_grad = pl.pallas_call(
        functools.partial(kernel, nz, nxc, ntp, cap, PLAN),
        out_shape=(
            jax.ShapeDtypeStruct(w_down.shape, bf16),
            jax.ShapeDtypeStruct((2, top, units, tokens), bf16),
            jax.ShapeDtypeStruct((top, tokens), f32),
        ),
        in_specs=[vmem] * 3 + [anywhere] * 3,
        out_specs=(anywhere,) * 2 + (vmem,),
        scratch_shapes=scratch,
        compiler_params=pltpu.CompilerParams(
            collective_id=0, has_side_effects=True, vmem_limit_bytes=56 * 1024 * 1024
        ),
    )(
        grad_out, routes.T, combine.T, jnp.transpose(gate_act, (1, 2, 0)),
        jnp.transpose(up_act, (1, 2, 0)), w_down,
    )
    return (
        w_grad,
        jnp.transpose(act_grad[0], (2, 0, 1)),
        jnp.transpose(act_grad[1], (2, 0, 1)),
        combine_grad.T,
    )


def solution(mesh, nz=16):
    placed = (
        P("ep", "tp"),
        P("ep", None),
        P("ep", None),
        P("ep", None, "tp"),
        P("ep", None, "tp"),
        P("ep", None, "tp"),
    )
    return jax.shard_map(
        functools.partial(body, nz, mesh.shape["ep"] // nz),
        mesh=mesh,
        in_specs=placed,
        out_specs=(P("ep", None, "tp"), P("ep", None, "tp"), P("ep", None, "tp"), P("ep", None)),
        check_vma=False,
    )
```

```python
import functools

import jax
import jax.numpy as jnp
from jax import lax
from jax.experimental import pallas as pl
from jax.experimental.pallas import tpu as pltpu
from jax.sharding import PartitionSpec as P

MESH = pl.DeviceIdType.MESH
NT = (((1,), (1,)), ((), ()))


def regroup(blocks, cap):
    count = len(blocks)
    lane = lax.broadcasted_iota(jnp.int32, blocks[0].shape, 1)
    lanes = blocks[0].shape[1]
    bit = 1
    while bit < count:
        high = (lane & (bit * cap)) != 0
        fresh = list(blocks)
        for low in range(count):
            if low & bit:
                continue
            a, b = blocks[low], blocks[low | bit]
            fresh[low] = jnp.where(high, pltpu.roll(b, bit * cap, 1), a)
            fresh[low | bit] = jnp.where(high, b, pltpu.roll(a, lanes - bit * cap, 1))
        blocks = fresh
        bit *= 2
    return blocks


def kernel(
    nz, nxc, ntp, cap, plan,
    grad, routes, combine, gate_in, up_in, w_in,
    wgrad_out, act_out, cg_out,
    gate, up, w, wgrad, rank,
    zbuf, sbuf, xs, rows, hs, rs, summed, xsend, xret, zsend, ret, wx, wxr, wz, wt, pick, wtok,
    fa, fb, fh, acc, gate_grad, up_grad, cgp, cgr,
    zg_s, zg_r, sl_s, sl_r, xs_s, xs_r, rs_s, rs_r, zr_s, zr_r, wx_s, wx_r, wz_s, wz_r, wy_s, wy_r,
    rx_s, rx_r, cg_s, cg_r, in_s, out_s,
):
    lag_project, lag_give, regroup_at, spread_each = plan
    tokens, feats = grad.shape
    top, units = gate.shape[0], gate.shape[1]
    experts = nz * nxc
    block = nxc * cap
    groups = nz // nxc
    wide = nxc * block
    near = nxc // 2
    half_z = nz // 2
    half_t = tokens // 2

    ep, y = lax.axis_index("ep"), lax.axis_index("tp")
    z, xc = ep // nxc, ep % nxc

    def at_z(other):
        return (other * nxc + xc, y)

    def at_xc(other):
        return (z * nxc + other, y)

    def at_y(other):
        return (ep, other)

    def remote(src, dst, send, recv, device):
        return pltpu.make_async_remote_copy(
            src_ref=src, dst_ref=dst, send_sem=send, recv_sem=recv, device_id=device,
            device_id_type=MESH,
        )

    def drain(ref, sem):
        pltpu.make_async_copy(ref, ref, sem).wait()

    def lanes_of(index):
        return pl.ds(pl.multiple_of(index * block, block), block)

    def rows_of(index):
        return pl.ds(pl.multiple_of(index * cap, cap), cap)

    def order(i, count=nz):
        return (count + jnp.where(i % 2 == 1, (i + 1) // 2, -(i // 2))) % count

    loads = [
        pltpu.make_async_copy(source, target, in_s.at[i])
        for i, (source, target) in enumerate(((gate_in, gate), (up_in, up), (w_in, w)))
    ]
    for load in loads:
        load.start()

    barrier = pltpu.get_barrier_semaphore()

    def greet(count, me, place):
        def one(i, _):
            d = order(i, count)
            pl.semaphore_signal(
                barrier, inc=1, device_id=place((me + d) % count), device_id_type=MESH
            )
            return 0

        lax.fori_loop(1, count, one, 0)

    greet(nz, z, at_z)
    greet(nxc, xc, at_xc)
    greet(ntp, y, at_y)
    pl.semaphore_wait(barrier, nz + nxc + ntp - 3)

    ahead = ((z + 1) % nz, (z + nz - 1) % nz)

    def ring(src, source, direction, step, part):
        span = pl.ds(part * half_t, half_t)
        return remote(
            src.at[span], zbuf.at[source, span], zg_s.at[direction, step, part],
            zg_r.at[direction, step, part], at_z(ahead[direction]),
        )

    def ring_slots(src, source, direction, step):
        return remote(
            src, sbuf.at[source], sl_s.at[direction, step], sl_r.at[direction, step],
            at_z(ahead[direction]),
        )

    for part in range(2):
        for direction in range(2):
            ring(grad, z, direction, 0, part).start()

    expert_of = lax.broadcasted_iota(jnp.int32, (experts, tokens), 0)
    named = jnp.zeros((experts, tokens), jnp.float32)
    for k in range(top):
        named = named + jnp.where(routes[k : k + 1, :] == expert_of, 1.0, 0.0)
    before = lax.broadcasted_iota(jnp.int32, (tokens, tokens), 0) < lax.broadcasted_iota(
        jnp.int32, (tokens, tokens), 1
    )
    rank[...] = jnp.dot(
        named.astype(jnp.bfloat16),
        jnp.where(before, 1.0, 0.0).astype(jnp.bfloat16),
        preferred_element_type=jnp.float32,
    )
    code = rank[...] + (expert_of * cap).astype(jnp.float32)
    for k in range(top):
        picked = jnp.where(routes[k : k + 1, :] == expert_of, code, 0.0)
        sbuf[z, k : k + 1, :] = jnp.sum(picked, axis=0, keepdims=True).astype(jnp.int32)
    for direction in range(2):
        ring_slots(sbuf.at[z], z, direction, 0).start()

    def deal(source, chunk):
        at = lax.broadcasted_iota(jnp.int32, (block, tokens), 0) + z * block
        chosen = sbuf[source, 0:1, :] == at
        for k in range(1, top):
            chosen = chosen | (sbuf[source, k : k + 1, :] == at)
        select = jnp.where(chosen, 1.0, 0.0).astype(jnp.bfloat16)
        piece = min(256, feats)
        for lo in range(0, feats, piece):
            xs[source, :, lo : lo + piece] = jnp.dot(
                select, chunk[:, lo : lo + piece], preferred_element_type=jnp.float32
            ).astype(jnp.bfloat16)
        rows[source, rows_of(xc), :] = xs[source, rows_of(xc), :]

        def send(d, _):
            other = (xc + d) % nxc
            remote(
                xs.at[source, rows_of(other)], rows.at[source, rows_of(xc)],
                xs_s.at[source], xs_r.at[source], at_xc(other),
            ).start()
            return 0

        lax.fori_loop(1, nxc, send, 0)

    deal(z, grad)
    loads[2].wait()

    def weigh(lower, upper):
        if lower == 0:
            loads[0].wait()
            loads[1].wait()
        away = (z - expert_of // nxc + near + nz) % nz
        base = away * block + (expert_of % nxc) * cap
        code = rank[...] + base.astype(jnp.float32)
        for k in range(lower, upper):
            picked = jnp.where(routes[k : k + 1, :] == expert_of, code, 0.0)
            slot = jnp.sum(picked, axis=0, keepdims=True).astype(jnp.int32)
            lanes = slice(k * tokens, (k + 1) * tokens)

            def mark(i, _):
                span = pl.ds(pl.multiple_of(i * block, block), block)
                at = lax.broadcasted_iota(jnp.int32, (block, tokens), 0) + i * block
                pick[span, lanes] = jnp.where(slot == at, 1.0, 0.0).astype(jnp.bfloat16)
                return 0

            lax.fori_loop(0, nz, mark, 0)

            g = gate[k].astype(jnp.float32)
            u = up[k].astype(jnp.float32)
            c = combine[k : k + 1, :]
            s = 1.0 / (1.0 + jnp.exp(-g))
            silu = g * s
            hidden = silu * u
            fh[k] = hidden
            fa[k] = c * u * s * (1.0 + g * (1.0 - s))
            fb[k] = c * silu
            wtok[:, lanes] = (c * hidden).astype(jnp.bfloat16)

    def place_weighted(i, _):
        part, pair = i // (nxc // 2), i % (nxc // 2)
        slots = [
            pick[rows_of((part * nxc + low) * nxc + 2 * pair + side), :]
            for side in range(2)
            for low in range(nxc)
        ]
        value = lax.dot_general(
            wtok[...], jnp.concatenate(slots, axis=0), NT, preferred_element_type=jnp.float32
        ).astype(jnp.bfloat16)
        wx[2 * pair, part] = value[:, :block]
        wx[2 * pair + 1, part] = value[:, block:]
        return 0

    def place(lower, upper):
        lax.fori_loop(lower * nxc // 2, upper * nxc // 2, place_weighted, 0)
        if upper < groups:
            return

        def send_wx(d, _):
            other = (xc + d) % nxc
            remote(wx.at[other], wxr.at[xc], wx_s, wx_r, at_xc(other)).start()
            return 0

        lax.fori_loop(1, nxc, send_wx, 0)
        wxr[xc] = wx[xc]

    strip = 16 if units % 16 == 0 else units

    def regroup_weighted():
        drain(wxr.at[pl.ds(0, nxc - 1)], wx_r)

        def one(i, _):
            span = pl.ds(pl.multiple_of(i * strip, strip), strip)
            for part in range(groups):
                blocks = [wxr[o, part, span, :].astype(jnp.float32) for o in range(nxc)]
                for low, value in enumerate(regroup(blocks, cap)):
                    wz[part * nxc + low, span, :] = value.astype(jnp.bfloat16)
            return 0

        lax.fori_loop(0, units // strip, one, 0)

    def send_weighted():
        def send(i, _):
            d = order(i)
            other = (z + d) % nz
            remote(
                wz.at[(near + nz - d) % nz], wt.at[y, :, lanes_of(z)], wz_s.at[other], wz_r.at[z],
                at_z(other),
            ).start()
            return 0

        lax.fori_loop(1, nz, send, 0)
        wt[y, :, lanes_of(z)] = wz[near]

    def spread_weighted(i, _):
        source = (z + nz - order(i)) % nz

        @pl.when(i > 0)
        def _():
            drain(wt.at[y, :, lanes_of(source)], wz_r.at[source])

        for e in range(1, ntp):
            remote(
                wt.at[y, :, lanes_of(source)], wt.at[y, :, lanes_of(source)], wy_s, wy_r,
                at_y((y + e) % ntp),
            ).start()
        return 0

    def project(source):
        drain(rows.at[source, pl.ds(0, block - cap)], xs_r.at[source])
        for d in range(ntp):
            other = (y + ntp - 1 - d) % ntp
            weights = w[0, pl.ds(pl.multiple_of(other * units, units), units), :]
            value = lax.dot_general(
                weights, rows[source], NT, preferred_element_type=jnp.float32
            ).astype(jnp.bfloat16)
            if d == ntp - 1:
                rs[source, y] = value
            else:
                hs[source, d] = value
                remote(
                    hs.at[source, d], rs.at[source, y], rs_s.at[source], rs_r.at[source],
                    at_y(other),
                ).start()

    def total(source):
        drain(rs.at[source, pl.ds(0, ntp - 1)], rs_r.at[source])
        out = rs[source, 0].astype(jnp.float32)
        for q in range(1, ntp):
            out = out + rs[source, q].astype(jnp.float32)
        return out.astype(jnp.bfloat16)

    def add_up(source):
        summed[(source - z + near + nz) % nz] = total(source)

    def regroup_group(part, take, put):
        def one(i, _):
            span = pl.ds(pl.multiple_of(i * strip, strip), strip)
            blocks = [take(low, span).astype(jnp.float32) for low in range(nxc)]
            for other, value in enumerate(regroup(blocks, cap)):
                put(other, span, value.astype(jnp.bfloat16))
            return 0

        lax.fori_loop(0, units // strip, one, 0)

    def return_x(part):
        def put(other, span, value):
            xsend[part, other, span, :] = value

        regroup_group(part, lambda low, span: summed[part * nxc + low, span, :], put)

        def send(d, _):
            other = (xc + d) % nxc
            remote(
                xsend.at[part, other], xret.at[part, xc], rx_s.at[part], rx_r.at[part],
                at_xc(other),
            ).start()
            return 0

        lax.fori_loop(1, nxc, send, 0)
        xret[part, xc] = xsend[part, xc]

    def return_z(part):
        drain(xret.at[part, pl.ds(0, nxc - 1)], rx_r.at[part])

        def put(low, span, value):
            zsend[part * nxc + low, span, :] = value

        regroup_group(part, lambda other, span: xret[part, other, span, :], put)

        def hops(low):
            away = abs(part * nxc + low - near)
            return -min(away, nz - away)

        for low in sorted(range(nxc), key=hops):
            index = part * nxc + low
            lanes = slice(low * block, (low + 1) * block)
            if index == near:
                ret[part, :, lanes] = zsend[index]
            else:
                remote(
                    zsend.at[index], ret.at[part, :, pl.ds(low * block, block)],
                    zr_s.at[index], zr_r.at[index], at_z((z + index - near + nz) % nz),
                ).start()

    def below(step):
        return (z + nz - step) % nz

    def above(step):
        return (z + step) % nz

    def both(step, act):
        act(below(step))
        act(above(step))

    def at_step(step, lag, own, act):
        @pl.when(step == lag)
        def _():
            own()

        @pl.when(step > lag)
        def _():
            both(step - lag, act)

    share = -(-top // 3)
    middle = groups // 2
    work = [
        (1, lambda: weigh(0, share)),
        (2, lambda: weigh(share, 2 * share)),
        (3, lambda: weigh(2 * share, top)),
        (half_z - 4, lambda: place(0, middle)),
        (half_z - 3, lambda: place(middle, groups)),
        (regroup_at, regroup_weighted),
    ]

    def gather_step(step, _):
        sources = (below(step), above(step))
        for part in range(2):
            for direction in range(2):
                source = sources[direction]
                ring(zbuf.at[source], source, direction, step - 1, part).wait_recv()
                if part == direction:
                    ring(zbuf.at[source], source, direction, step, part).start()
                else:

                    @pl.when(step < half_z - 1)
                    def _():
                        ring(zbuf.at[source], source, direction, step, part).start()

        for direction in range(2):
            source = sources[direction]
            ring_slots(sbuf.at[source], source, direction, step - 1).wait_recv()
            if direction == 0:
                ring_slots(sbuf.at[source], source, direction, step).start()
            else:

                @pl.when(step < half_z - 1)
                def _():
                    ring_slots(sbuf.at[source], source, direction, step).start()

        for direction in range(2):
            deal(sources[direction], zbuf.at[sources[direction]])

        at_step(step, lag_project, lambda: project(z), project)
        at_step(step, lag_give, lambda: add_up(z), add_up)

        for at, act in work:

            @pl.when(step == at)
            def _():
                act()

        return 0

    lax.fori_loop(1, half_z, gather_step, 0)

    def late(step, lag, own, act):
        at = step - lag
        if at == 0:
            own()
        elif 0 < at < half_z:
            both(at, act)
        elif at == half_z:
            act(far)

    def spread(count):
        upto = min(nz, spread_to[-1] + count)
        lax.fori_loop(spread_to[-1], upto, spread_weighted, 0)
        spread_to.append(upto)

    spread_to = [0]
    early = lag_give + near < half_z
    if regroup_at >= half_z:
        regroup_weighted()
    send_weighted()
    if early:
        return_x(0)

    far = above(half_z)
    for direction in range(2):
        ring(zbuf.at[far], far, direction, half_z - 1, direction).wait_recv()
    ring_slots(sbuf.at[far], far, 0, half_z - 1).wait_recv()
    deal(far, zbuf.at[far])

    for step in range(half_z, half_z + lag_give + 1):
        late(step, lag_project, lambda: project(z), project)
        late(step, lag_give, lambda: add_up(z), add_up)
        if step == half_z + (lag_project if early else lag_give):
            if not early:
                return_x(0)
            return_z(0)
        spread(spread_each[min(step - half_z, len(spread_each) - 2)])
    for part in range(1, groups):
        return_x(part)
    spread(spread_each[-1])
    for part in range(1, groups):
        return_z(part)
    spread(nz)

    drain(wt.at[pl.ds(0, ntp - 1)], wy_r)
    piece = min(256, feats)
    per = feats // piece

    def weight_gradient(i, _):
        q, n = i // per, i % per
        cols = pl.ds(pl.multiple_of(n * piece, piece), piece)
        wgrad[0, pl.ds(pl.multiple_of(q * units, units), units), cols] = jnp.dot(
            wt[q],
            rows[:, :, cols].reshape(nz * block, piece),
            preferred_element_type=jnp.float32,
        ).astype(jnp.bfloat16)
        return 0

    lax.fori_loop(0, ntp * per, weight_gradient, 0)
    store = pltpu.make_async_copy(wgrad, wgrad_out, out_s.at[0])
    store.start()

    pair = min(2, top) * tokens

    def collect(part):
        for low in range(nxc):
            index = part * nxc + low
            if index != near:
                drain(zsend.at[index], zr_r.at[index])

        def one(i, _):
            cols = pl.ds(pl.multiple_of(i * pair, pair), pair)
            value = jnp.dot(
                ret[part], pick[part * wide : (part + 1) * wide, cols],
                preferred_element_type=jnp.float32,
            )
            acc[:, cols] = value if part == 0 else acc[:, cols] + value
            return 0

        lax.fori_loop(0, top * tokens // pair, one, 0)

    for part in range(groups - 1):
        collect(part)

    for direction in range(2):
        for step in range(half_z):
            for part in range(2):
                if step < half_z - 1 or part == direction:
                    ring(grad, z, direction, step, part).wait_send()
            if step < half_z - 1 or direction == 0:
                ring_slots(sbuf.at[z], z, direction, step).wait_send()

    def settle(d, _):
        source = (z + d) % nz
        drain(xs.at[source, pl.ds(0, block - cap)], xs_s.at[source])
        drain(hs.at[source], rs_s.at[source])

        @pl.when(d > 0)
        def _():
            drain(wz.at[source], wz_s.at[source])

        return 0

    lax.fori_loop(0, nz, settle, 0)
    drain(wx.at[pl.ds(0, nxc - 1)], wx_s)
    drain(wt.at[pl.ds(0, ntp - 1)], wy_s)
    for part in range(groups):
        drain(xsend.at[part, pl.ds(0, nxc - 1)], rx_s.at[part])
    for index in range(nz):
        if index != near:
            drain(zsend.at[index], zr_s.at[index])
    collect(groups - 1)

    for k in range(top):
        raw = acc[:, k * tokens : (k + 1) * tokens]
        cgp[k : k + 1, :] = jnp.sum(fh[k] * raw, axis=0, keepdims=True)
    for e in range(1, ntp):
        remote(cgp, cgr.at[y], cg_s, cg_r, at_y((y + e) % ntp)).start()
    cgr[y] = cgp[...]
    for k in range(top):
        raw = acc[:, k * tokens : (k + 1) * tokens]
        gate_grad[k] = (fa[k] * raw).astype(jnp.bfloat16)
        up_grad[k] = (fb[k] * raw).astype(jnp.bfloat16)
    stores = [
        store,
        pltpu.make_async_copy(gate_grad, act_out.at[0], out_s.at[1]),
        pltpu.make_async_copy(up_grad, act_out.at[1], out_s.at[2]),
    ]
    stores[1].start()
    stores[2].start()
    drain(cgr.at[pl.ds(0, ntp - 1)], cg_s)
    drain(cgr.at[pl.ds(0, ntp - 1)], cg_r)
    router = cgr[0]
    for q in range(1, ntp):
        router = router + cgr[q]
    cg_out[...] = router
    for copy in stores:
        copy.wait()


PLAN = (2, 3, 8, (0, 0, 0, 4, 4))


def body(nz, nxc, grad_out, routes, combine, gate_act, up_act, w_down):
    tokens, top = routes.shape
    feats = grad_out.shape[1]
    units = gate_act.shape[2]
    ntp = lax.axis_size("tp")
    cap = 2 * tokens * top // (nz * nxc)
    block, groups = nxc * cap, nz // nxc
    half_z = nz // 2
    bf16, f32, i32 = jnp.bfloat16, jnp.float32, jnp.int32
    dma = pltpu.SemaphoreType.DMA
    vmem = pl.BlockSpec(memory_space=pltpu.VMEM)
    anywhere = pl.BlockSpec(memory_space=pl.ANY)
    scratch = [
        pltpu.VMEM((top, units, tokens), bf16),
        pltpu.VMEM((top, units, tokens), bf16),
        pltpu.VMEM(w_down.shape, bf16),
        pltpu.VMEM(w_down.shape, bf16),
        pltpu.VMEM((nz * nxc, tokens), f32),
        pltpu.VMEM((nz, tokens, feats), bf16),
        pltpu.VMEM((nz, top, tokens), i32),
        pltpu.VMEM((nz, block, feats), bf16),
        pltpu.VMEM((nz, block, feats), bf16),
        pltpu.VMEM((nz, ntp - 1, units, block), bf16),
        pltpu.VMEM((nz, ntp, units, block), bf16),
        pltpu.VMEM((nz, units, block), bf16),
        pltpu.VMEM((groups, nxc, units, block), bf16),
        pltpu.VMEM((groups, nxc, units, block), bf16),
        pltpu.VMEM((nz, units, block), bf16),
        pltpu.VMEM((groups, units, nxc * block), bf16),
        pltpu.VMEM((nxc, groups, units, block), bf16),
        pltpu.VMEM((nxc, groups, units, block), bf16),
        pltpu.VMEM((nz, units, block), bf16),
        pltpu.VMEM((ntp, units, nz * block), bf16),
        pltpu.VMEM((nz * block, top * tokens), bf16),
        pltpu.VMEM((units, top * tokens), bf16),
        pltpu.VMEM((top, units, tokens), f32),
        pltpu.VMEM((top, units, tokens), f32),
        pltpu.VMEM((top, units, tokens), f32),
        pltpu.VMEM((units, top * tokens), f32),
        pltpu.VMEM((top, units, tokens), bf16),
        pltpu.VMEM((top, units, tokens), bf16),
        pltpu.VMEM((top, tokens), f32),
        pltpu.VMEM((ntp, top, tokens), f32),
        dma((2, half_z, 2)), dma((2, half_z, 2)), dma((2, half_z)), dma((2, half_z)),
        dma((nz,)), dma((nz,)), dma((nz,)), dma((nz,)), dma((nz,)), dma((nz,)),
        dma(()), dma(()), dma((nz,)), dma((nz,)), dma(()), dma(()),
        dma((groups,)), dma((groups,)), dma(()), dma(()), dma((3,)), dma((3,)),
    ]
    w_grad, act_grad, combine_grad = pl.pallas_call(
        functools.partial(kernel, nz, nxc, ntp, cap, PLAN),
        out_shape=(
            jax.ShapeDtypeStruct(w_down.shape, bf16),
            jax.ShapeDtypeStruct((2, top, units, tokens), bf16),
            jax.ShapeDtypeStruct((top, tokens), f32),
        ),
        in_specs=[vmem] * 3 + [anywhere] * 3,
        out_specs=(anywhere,) * 2 + (vmem,),
        scratch_shapes=scratch,
        compiler_params=pltpu.CompilerParams(
            collective_id=0, has_side_effects=True, vmem_limit_bytes=56 * 1024 * 1024
        ),
    )(
        grad_out, routes.T, combine.T, jnp.transpose(gate_act, (1, 2, 0)),
        jnp.transpose(up_act, (1, 2, 0)), w_down,
    )
    return (
        w_grad,
        jnp.transpose(act_grad[0], (2, 0, 1)),
        jnp.transpose(act_grad[1], (2, 0, 1)),
        combine_grad.T,
    )


def solution(mesh, nz=16):
    placed = (
        P("ep", "tp"),
        P("ep", None),
        P("ep", None),
        P("ep", None, "tp"),
        P("ep", None, "tp"),
        P("ep", None, "tp"),
    )
    return jax.shard_map(
        functools.partial(body, nz, mesh.shape["ep"] // nz),
        mesh=mesh,
        in_specs=placed,
        out_specs=(P("ep", None, "tp"), P("ep", None, "tp"), P("ep", None, "tp"), P("ep", None)),
        check_vma=False,
    )
```
